32 devices in a mesh: blk: 8 (over y, x, core), grp: 4 (over z).
Axes of the slice: x: 2, y: 2, z: 4, core: 2. Of those that a mesh axis runs over, the one named last changes fastest.
Arguments:
- amplitudes: bfloat16 [1024, 8, 4, 128], P('blk'), may hold values from -6 to 6
- integrals: bfloat16 [256, 1024, 128], P('grp', 'blk'), may hold values from -0.15625 to 0.15625
- virt_energy: float32 [1024], replicated, may hold values from 0.5 to 4
- pair_energy: float32 [8], replicated, may hold values from -3 to -0.5
- offsets: int32 [8, 4], replicated, may hold values from 0 to 7, as said below
Outputs:
- ladder: float32 [1024, 8, 4, 128], P(('blk', 'grp'))
- new_amplitudes: float32 [1024, 8, 4, 128], P(('blk', 'grp'))
The draws below stay inside these ranges and needn't reach their ends.
Inputs may be any that keep to these rules, and one draw needn't show every extreme that they name: The 4 offsets of one row tile are different; the first 3 are at most 2, the last is larger than 2.
All inputs are finite; a program needn't handle non-finite values.
Results may differ from the reference program's by a relative error of at most 0.0029.
Values may be sent and summed in bfloat16 or wider, within the bound.
A program may use at most 64 MiB of HBM per device.

```python
import math
import jax
import jax.numpy as jnp
from jax import lax

VT = 128
NAUX = 256
NPAIR = 8
SLOTS = 4
DMAX = 2
NT = 8
NV = 1024


def draw_offsets(key, part):
    values = jnp.arange(DMAX + 1, dtype=jnp.int32)
    rows = jnp.arange(NT, dtype=jnp.int32)
    scores = jax.random.randint(key, (NT, DMAX + 1), 0, 1 << 20, dtype=jnp.int32) * (DMAX + 1) + values[None, :]
    forced = jax.random.randint(jax.random.fold_in(key, 7), (), 0, NT, dtype=jnp.int32)
    on_row = rows[:, None] == forced
    scores = jnp.where(on_row & (values[None, :] == 0), -1, scores)
    order = jnp.argsort(scores, axis=1, stable=True)[:, :SLOTS - 1]
    far_draw = jax.random.randint(jax.random.fold_in(key, 11), (NT,), DMAX + 1, NT, dtype=jnp.int32)
    far_draw = jnp.where(rows == forced, NT // 2, far_draw)
    far_draw = jnp.where(rows == (forced + 1) % NT, NT - 1, far_draw)
    return jnp.concatenate([order.astype(jnp.int32), far_draw[:, None].astype(jnp.int32)], axis=1)


def steps_of(stream_key, dims, shards, smallest, high):
    def one(position, shards_of):
        heights = jax.random.uniform(jax.random.fold_in(jax.random.fold_in(stream_key, 6), position), (shards_of,), jnp.float32, smallest / len(shards), high / len(shards))
        return jnp.repeat(jnp.exp(heights), dims[position] // shards_of).reshape((-1,) + (1,) * (len(dims) - position - 1))

    factor_of = one(*shards[0])
    for cut in shards[1:]:
        factor_of = factor_of * one(*cut)
    return factor_of


def gaussian(stream_key, shape, width, bound, shards=(), kind=jnp.bfloat16):
    result = width * jax.random.normal(stream_key, shape, jnp.float32)
    if shards:
        result = result * steps_of(stream_key, shape, shards, -0.22, 0.18)
    return jnp.clip(result, -bound, bound).astype(kind)


def setup_inputs(seed: int = 0) -> dict:
    key_list = jax.random.split(jax.random.key(seed), 6)
    amplitudes = gaussian(key_list[0], (NV, NPAIR, SLOTS, VT), 1.0, 6.0, ((0, 8),))
    integrals = gaussian(key_list[1], (NAUX, NV, VT), (VT * 11) ** -0.5, 0.15625, ((0, 4), (1, 8)))
    virt_energy = jnp.clip(jnp.exp(jax.random.uniform(key_list[2], (NV,), jnp.float32, math.log(0.5), math.log(4.0))), 0.5, 4.0)
    pair_energy = jnp.clip(jax.random.uniform(key_list[3], (NPAIR,), jnp.float32, -3.0, -0.5), -3.0, -0.5)
    offsets = draw_offsets(jax.random.fold_in(key_list[5], 71), 0)
    return {"amplitudes": amplitudes, "integrals": integrals, "virt_energy": virt_energy, "pair_energy": pair_energy, "offsets": offsets}


def reference(amplitudes, integrals, virt_energy, pair_energy, offsets):
    ntile = NV // VT
    amp = amplitudes.reshape(ntile, VT, NPAIR * SLOTS * VT)
    blocks = integrals.reshape(NAUX, ntile, VT, VT)
    rows = jnp.arange(ntile, dtype=jnp.int32)
    cols = ((rows[:, None] - offsets) % ntile).astype(jnp.int32)

    def one_tile(k):
        own = blocks[:, k]
        col_blocks = jnp.take(blocks, cols[k], axis=1)
        amp_tile = amp[k]

        def add_aux(total, q):
            half_split = jnp.dot(own[q], amp_tile, preferred_element_type=jnp.float32).astype(jnp.bfloat16)
            half_split = lax.optimization_barrier(half_split).astype(jnp.float32).reshape(VT, NPAIR, SLOTS, VT)
            term = jnp.einsum("apsd,sbd->apsb", half_split, col_blocks[q].astype(jnp.float32))
            return total + term, None

        start = jnp.zeros((VT, NPAIR, SLOTS, VT), jnp.float32)
        total, _ = lax.scan(add_aux, start, jnp.arange(NAUX, dtype=jnp.int32))
        return total

    ladder = lax.map(one_tile, rows)
    table = virt_energy.reshape(ntile, VT)
    col_energy = table[cols]
    denom = (table[:, :, None, None, None] + col_energy[:, None, None, :, :]
             - pair_energy[None, None, :, None, None])
    old = amplitudes.astype(jnp.float32).reshape(ntile, VT, NPAIR, SLOTS, VT)
    new_amplitudes = old - ladder / denom
    return (ladder.reshape(NV, NPAIR, SLOTS, VT), new_amplitudes.reshape(NV, NPAIR, SLOTS, VT))
```

```python
import functools

import jax
import jax.numpy as jnp
from jax import lax
from jax.experimental import pallas as pl
from jax.experimental.pallas import tpu as pltpu
from jax.sharding import PartitionSpec as P

MESH = pl.DeviceIdType.MESH
GROUP = 4


def grid_of(chips):
    rows = max(d for d in range(1, chips + 1) if chips % d == 0 and d * d <= chips)
    return rows, chips // rows


def kernel(tiles, groups, chunks, sel_ref, amp_ref, int_ref, out_ref, *scratch):
    gath = scratch[:chunks]
    acc, out_buf, in_buf, send_sem, recv_sem, red_send, red_recv = scratch[chunks:]
    rows_of, cols_of = grid_of(tiles // 2)
    slots = amp_ref.shape[0]
    aux, width = int_ref.shape[0], int_ref.shape[1]
    pairs = amp_ref.shape[2] // width
    share = width // groups
    depth = aux // chunks
    part = depth // 2

    me = lax.axis_index("blk")
    grp = lax.axis_index("grp")
    core = lax.rem(me, 2)
    chip = me // 2
    hi = chip // cols_of
    lo = lax.rem(chip, cols_of)

    def tile_at(dy, dx, other=False):
        y = lax.rem(hi + dy, rows_of)
        x = lax.rem(lo + dx, cols_of)
        return (y * cols_of + x) * 2 + ((1 - core) if other else core)

    sibling = tile_at(0, 0, True)
    steps_y, steps_x = range(1, rows_of), range(1, cols_of)
    friends = [sibling] + [tile_at(0, d) for d in steps_x] + [tile_at(d, 0) for d in steps_y]

    barrier = pltpu.get_barrier_semaphore()
    for friend in friends:
        pl.semaphore_signal(barrier, inc=1, device_id={"blk": friend}, device_id_type=MESH)
    for d in range(1, groups):
        pl.semaphore_signal(
            barrier, inc=1, device_id={"grp": lax.rem(grp + d, groups)}, device_id_type=MESH
        )
    pl.semaphore_wait(barrier, len(friends) + groups - 1)

    sent = []

    def piece(c, tile, h):
        return gath[c].at[tile, pl.ds(h * part, part)]

    def send(src, c, tile, h, to):
        copy = pltpu.make_async_remote_copy(
            src_ref=src,
            dst_ref=piece(c, tile, h),
            send_sem=send_sem.at[len(sent)],
            recv_sem=recv_sem.at[tile, c, h],
            device_id={"blk": to},
            device_id_type=MESH,
        )
        copy.start()
        sent.append(copy)

    def arrived(c, tile, h):
        pltpu.make_async_remote_copy(
            src_ref=piece(c, tile, h),
            dst_ref=piece(c, tile, h),
            send_sem=send_sem.at[0],
            recv_sem=recv_sem.at[tile, c, h],
            device_id={"blk": sibling},
            device_id_type=MESH,
        ).wait_recv()

    def send_own(c):
        src = [int_ref.at[pl.ds(c * depth + h * part, part)] for h in (0, 1)]
        for h in (0, 1):
            for d in steps_x:
                send(src[h], c, me, h, tile_at(0, d))
            for d in steps_y:
                send(src[1 - h], c, me, 1 - h, tile_at(d, 0))
        for h in (0, 1):
            send(src[h], c, me, h, sibling)

    def relay(c):
        for first in (True, False):
            for d in steps_x:
                tile, h = tile_at(0, cols_of - d), 0 if first else 1
                arrived(c, tile, h)
                if first:
                    for e in steps_y:
                        send(piece(c, tile, h), c, tile, h, tile_at(e, 0))
                send(piece(c, tile, h), c, tile, h, sibling)
            for d in steps_y:
                tile, h = tile_at(rows_of - d, 0), 1 if first else 0
                arrived(c, tile, h)
                if first:
                    for e in steps_x:
                        send(piece(c, tile, h), c, tile, h, tile_at(0, e))
                send(piece(c, tile, h), c, tile, h, sibling)

    def hand_over(c):
        for h in (0, 1):
            for dy in steps_y:
                for dx in steps_x:
                    tile = tile_at(dy, dx)
                    arrived(c, tile, h)
                    send(piece(c, tile, h), c, tile, h, sibling)

    def from_sibling(c):
        for h in (0, 1):
            for dy in range(rows_of):
                for dx in range(cols_of):
                    arrived(c, tile_at(dy, dx, True), h)

    def work(c, order, slot, column):
        def body(i, _):
            first = i * GROUP
            own = int_ref[pl.ds(c * depth + first, GROUP)].reshape(GROUP * width, width)
            half = jnp.dot(own, amp_ref[slot], preferred_element_type=jnp.float32)
            half = half.astype(jnp.bfloat16)
            left = jnp.concatenate(
                [
                    jnp.concatenate(
                        [
                            half[g * width:(g + 1) * width, p * width:(p + 1) * width]
                            for g in range(GROUP)
                        ],
                        axis=1,
                    )
                    for p in range(pairs)
                ],
                axis=0,
            )
            block = column(first)
            right = jnp.concatenate([block[g] for g in range(GROUP)], axis=1)
            term = lax.dot_general(
                left, right, (((1,), (1,)), ((), ())), preferred_element_type=jnp.float32
            ).reshape(pairs, width, width)
            acc[order] += term
            return 0

        lax.fori_loop(0, depth // GROUP, body, 0)

    def reduce_copy(d, order):
        return pltpu.make_async_remote_copy(
            src_ref=out_buf.at[d - 1, order],
            dst_ref=in_buf.at[d - 1, order],
            send_sem=red_send.at[d - 1, order],
            recv_sem=red_recv.at[d - 1, order],
            device_id={"grp": lax.rem(grp + d, groups)},
            device_id_type=MESH,
        )

    def reduce_send(order):
        for d in range(1, groups):
            to = lax.rem(grp + d, groups)
            rows = acc[order, :, pl.ds(to * share, share), :].reshape(pairs * share, width)
            out_buf[d - 1, order] = rows.astype(jnp.bfloat16)
            reduce_copy(d, order).start()

    slot_of = [sel_ref[0, o] for o in range(slots)]
    far = sel_ref[1, slots - 1]

    send_own(0)
    if chunks > 1:
        send_own(1)
    acc[...] = jnp.zeros_like(acc)
    for c in range(chunks + 1):
        if c < chunks:
            work(c, 0, slot_of[0], lambda f: int_ref[pl.ds(c * depth + f, GROUP)])
            relay(c)
            if c + 2 < chunks:
                send_own(c + 2)
            if c == chunks - 1:
                reduce_send(0)
        if c > 0:
            b = c - 1
            hand_over(b)
            from_sibling(b)
            for o in range(1, slots - 1):
                near = lax.rem(me + tiles - o, tiles)
                work(b, o, slot_of[o], lambda f: gath[b][near, pl.ds(f, GROUP)])
                if b == chunks - 1:
                    reduce_send(o)
            work(b, slots - 1, slot_of[slots - 1], lambda f: gath[b][far, pl.ds(f, GROUP)])
    reduce_send(slots - 1)
    for copy in sent:
        copy.wait_send()
    for o in range(slots):
        for d in range(1, groups):
            reduce_copy(d, o).wait()
    for s in range(slots):
        o = sel_ref[2, s]
        total = acc[o, :, pl.ds(grp * share, share), :].reshape(pairs * share, width)
        for d in range(1, groups):
            total = total + in_buf[d - 1, o].astype(jnp.float32)
        out_ref[s] = total


def local(tiles, groups, amplitudes, integrals, virt_energy, pair_energy, offsets):
    tile_index = lax.axis_index("blk")
    group_index = lax.axis_index("grp")
    aux, width = integrals.shape[0], integrals.shape[2]
    pairs, slots = amplitudes.shape[1], amplitudes.shape[2]
    share = width // groups
    chunks = max(2, min(4, 32 // tiles))
    own_offsets = lax.dynamic_slice_in_dim(offsets, tile_index, 1, 0)[0]
    cols = (tile_index - own_offsets) % tiles
    ids = jnp.arange(slots, dtype=jnp.int32)
    place = jnp.where(ids == slots - 1, slots - 1, own_offsets)
    slot_of = jnp.sum(jnp.where(place[None, :] == ids[:, None], ids[None, :], 0), axis=1)
    select = jnp.stack([slot_of, jnp.broadcast_to(cols[slots - 1], (slots,)), place])
    select = select.astype(jnp.int32)
    by_slot = amplitudes.transpose(2, 0, 1, 3).reshape(slots, width, pairs * width)

    rows_of, cols_of = grid_of(tiles // 2)
    y, x = rows_of - 1, cols_of - 1
    n_sent = chunks * (2 * (1 + x + y) + 2 * x * y + 2 * (x + y + x * y))
    depth = aux // chunks
    summed = pl.pallas_call(
        functools.partial(kernel, tiles, groups, chunks),
        out_shape=jax.ShapeDtypeStruct((slots, pairs * share, width), jnp.float32),
        in_specs=[
            pl.BlockSpec(memory_space=pltpu.SMEM),
            pl.BlockSpec(memory_space=pltpu.VMEM),
            pl.BlockSpec(memory_space=pltpu.VMEM),
        ],
        out_specs=pl.BlockSpec(memory_space=pltpu.VMEM),
        scratch_shapes=[pltpu.VMEM((tiles, depth, width, width), jnp.bfloat16)] * chunks
        + [
            pltpu.VMEM((slots, pairs, width, width), jnp.float32),
            pltpu.VMEM((groups - 1, slots, pairs * share, width), jnp.bfloat16),
            pltpu.VMEM((groups - 1, slots, pairs * share, width), jnp.bfloat16),
            pltpu.SemaphoreType.DMA((n_sent,)),
            pltpu.SemaphoreType.DMA((tiles, chunks, 2)),
            pltpu.SemaphoreType.DMA((groups - 1, slots)),
            pltpu.SemaphoreType.DMA((groups - 1, slots)),
        ],
        compiler_params=pltpu.CompilerParams(
            collective_id=0, has_side_effects=True, vmem_limit_bytes=56 << 20
        ),
        cost_estimate=pl.CostEstimate(
            flops=4 * aux * slots * pairs * width**3,
            bytes_accessed=4 << 20,
            transcendentals=0,
        ),
    )(select, by_slot, integrals)
    ladder = summed.reshape(slots, pairs, share, width).transpose(2, 1, 0, 3)

    first_row = group_index * share
    old_rows = lax.dynamic_slice_in_dim(amplitudes, first_row, share, 0).astype(jnp.float32)
    row_energy = lax.dynamic_slice_in_dim(virt_energy, tile_index * width + first_row, share, 0)
    table = virt_energy.reshape(tiles, width)
    col_energy = jnp.stack(
        [lax.dynamic_index_in_dim(table, cols[s], 0, keepdims=False) for s in range(slots)]
    )
    denom = (
        row_energy[:, None, None, None]
        + col_energy[None, None, :, :]
        - pair_energy[None, :, None, None]
    )
    return ladder, old_rows - ladder / denom


def solution(mesh):
    placed = (P("blk", None, None, None), P("grp", "blk", None), P(), P(), P())
    return jax.shard_map(
        functools.partial(local, mesh.shape["blk"], mesh.shape["grp"]),
        mesh=mesh,
        in_specs=placed,
        out_specs=(P(("blk", "grp"), None, None, None), P(("blk", "grp"), None, None, None)),
        check_vma=False,
    )
```

```python
import functools

import jax
import jax.numpy as jnp
from jax import lax
from jax.experimental import pallas as pl
from jax.experimental.pallas import tpu as pltpu
from jax.sharding import PartitionSpec as P

MESH = pl.DeviceIdType.MESH
GROUP = 4


def grid_of(chips):
    rows = max(d for d in range(1, chips + 1) if chips % d == 0 and d * d <= chips)
    return rows, chips // rows


def kernel(tiles, groups, chunks, off_ref, table_ref, raw_ref, int_ref, out_ref, col_ref, *scratch):
    gath = scratch[:chunks]
    amp_ref, acc, out_buf, in_buf, send_sem, recv_sem, red_send, red_recv = scratch[chunks:]
    rows_of, cols_of = grid_of(tiles // 2)
    slots = raw_ref.shape[2]
    aux, width = int_ref.shape[0], int_ref.shape[1]
    pairs = raw_ref.shape[1]
    share = width // groups
    depth = aux // chunks
    part = depth // 2

    me = lax.axis_index("blk")
    grp = lax.axis_index("grp")
    core = lax.rem(me, 2)
    chip = me // 2
    hi = chip // cols_of
    lo = lax.rem(chip, cols_of)

    def tile_at(dy, dx, other=False):
        y = lax.rem(hi + dy, rows_of)
        x = lax.rem(lo + dx, cols_of)
        return (y * cols_of + x) * 2 + ((1 - core) if other else core)

    sibling = tile_at(0, 0, True)
    steps_y, steps_x = range(1, rows_of), range(1, cols_of)
    friends = [sibling] + [tile_at(0, d) for d in steps_x] + [tile_at(d, 0) for d in steps_y]

    barrier = pltpu.get_barrier_semaphore()
    for friend in friends:
        pl.semaphore_signal(barrier, inc=1, device_id={"blk": friend}, device_id_type=MESH)
    for d in range(1, groups):
        pl.semaphore_signal(
            barrier, inc=1, device_id={"grp": lax.rem(grp + d, groups)}, device_id_type=MESH
        )
    pl.semaphore_wait(barrier, len(friends) + groups - 1)

    sent = {}
    near_x = lo != 0

    def piece(c, tile, h):
        return gath[c].at[tile, pl.ds(h * part, part)]

    def send_copy(key, own, c, at, h, to):
        tile = tile_at(*at)
        src = int_ref.at[pl.ds(c * depth + h * part, part)] if own else piece(c, tile, h)
        return pltpu.make_async_remote_copy(
            src_ref=src,
            dst_ref=piece(c, tile, h),
            send_sem=send_sem.at[sent[key]],
            recv_sem=recv_sem.at[tile, c, h],
            device_id={"blk": tile_at(*to)},
            device_id_type=MESH,
        )

    def send(own, c, at, h, to):
        key = (own, c, at, h, to)
        sent.setdefault(key, len(sent))
        send_copy(key, *key).start()

    def arrived(c, at, h):
        tile = tile_at(*at)
        pltpu.make_async_remote_copy(
            src_ref=piece(c, tile, h),
            dst_ref=piece(c, tile, h),
            send_sem=send_sem.at[0],
            recv_sem=recv_sem.at[tile, c, h],
            device_id={"blk": sibling},
            device_id_type=MESH,
        ).wait_recv()

    to_sibling = (0, 0, True)
    peers_x = [(0, d) for d in steps_x]
    peers_y = [(d, 0) for d in steps_y]
    diagonal = [(dy, dx) for dy in steps_y for dx in steps_x]

    def send_x(c, h):
        for to in peers_x:
            send(True, c, (0, 0), h, to)

    def send_y(c, h):
        for to in peers_y:
            send(True, c, (0, 0), h, to)

    def pass_on(c, places, h):
        for at in places:
            arrived(c, at, h)
            send(False, c, at, h, to_sibling)

    def relay(c):
        for at in peers_x:
            arrived(c, at, 0)
            for to in peers_y:
                send(False, c, at, 0, to)
            send(False, c, at, 0, to_sibling)
        for at in peers_y:
            arrived(c, at, 1)
            for to in peers_x:
                send(False, c, at, 1, to)
            send(False, c, at, 1, to_sibling)

    def from_sibling(c, places):
        for at in places:
            for h in (0, 1):
                arrived(c, at + (True,), h)

    def near_arrivals(c):
        @pl.when(near_x)
        def _():
            pass_on(c, peers_x, 1)
            from_sibling(c, peers_x)

        @pl.when(jnp.logical_not(near_x))
        def _():
            pass_on(c, diagonal, 0)
            pass_on(c, diagonal, 1)
            from_sibling(c, diagonal)

        from_sibling(c, [(0, 0)])

    def far_arrivals(c):
        @pl.when(near_x)
        def _():
            pass_on(c, diagonal, 0)
            pass_on(c, diagonal, 1)

        @pl.when(jnp.logical_not(near_x))
        def _():
            pass_on(c, peers_x, 1)

        pass_on(c, peers_y, 0)

        @pl.when(near_x)
        def _():
            from_sibling(c, diagonal)

        @pl.when(jnp.logical_not(near_x))
        def _():
            from_sibling(c, peers_x)

        from_sibling(c, peers_y)

    def work(c, order, slot, column):
        def body(i, _):
            first = i * GROUP
            own = int_ref[pl.ds(c * depth + first, GROUP)].reshape(GROUP * width, width)
            half = jnp.dot(own, amp_ref[slot], preferred_element_type=jnp.float32)
            half = half.astype(jnp.bfloat16)
            left = jnp.concatenate(
                [
                    jnp.concatenate(
                        [
                            half[g * width:(g + 1) * width, p * width:(p + 1) * width]
                            for g in range(GROUP)
                        ],
                        axis=1,
                    )
                    for p in range(pairs)
                ],
                axis=0,
            )
            block = column(first)
            right = jnp.concatenate([block[g] for g in range(GROUP)], axis=1)
            term = lax.dot_general(
                left, right, (((1,), (1,)), ((), ())), preferred_element_type=jnp.float32
            ).reshape(pairs, width, width)
            acc[order] += term
            return 0

        lax.fori_loop(0, depth // GROUP, body, 0)

    def reduce_copy(d, order):
        return pltpu.make_async_remote_copy(
            src_ref=out_buf.at[d - 1, order],
            dst_ref=in_buf.at[d - 1, order],
            send_sem=red_send.at[d - 1, order],
            recv_sem=red_recv.at[d - 1, order],
            device_id={"grp": lax.rem(grp + d, groups)},
            device_id_type=MESH,
        )

    def reduce_send(order):
        for d in range(1, groups):
            to = lax.rem(grp + d, groups)
            rows = acc[order, :, pl.ds(to * share, share), :].reshape(pairs * share, width)
            out_buf[d - 1, order] = rows.astype(jnp.bfloat16)
            reduce_copy(d, order).start()

    place = [off_ref[s, me] for s in range(slots - 1)]
    slot_of = [
        sum((jnp.where(place[s] == o, s, 0) for s in range(1, slots - 1)), 0)
        for o in range(slots - 1)
    ] + [slots - 1]
    place = place + [slots - 1]
    far = lax.rem(me - off_ref[slots - 1, me] + tiles, tiles)

    for c in range(chunks):
        send_x(c, 0)
        send_y(c, 1)
        for h in (0, 1):
            send(True, c, (0, 0), h, to_sibling)

    @pl.when(jnp.logical_not(near_x))
    def _():
        for c in range(chunks):
            send_x(c, 1)

    for s in range(slots):
        for p in range(pairs):
            amp_ref[s, :, p * width:(p + 1) * width] = raw_ref[:, p, s, :]
    acc[...] = jnp.zeros_like(acc)
    for c in range(chunks):
        work(c, 0, slot_of[0], lambda f: int_ref[pl.ds(c * depth + f, GROUP)])
        relay(c)

    @pl.when(near_x)
    def _():
        for c in range(chunks):
            send_x(c, 1)

    for c in range(chunks):
        send_y(c, 0)
    reduce_send(0)
    for c in range(chunks):
        near_arrivals(c)
        for o in range(1, slots - 1):
            near = lax.rem(me + tiles - o, tiles)
            work(c, o, slot_of[o], lambda f: gath[c][near, pl.ds(f, GROUP)])
            if c == chunks - 1:
                reduce_send(o)
    for c in range(chunks):
        far_arrivals(c)
        work(c, slots - 1, slots - 1, lambda f: gath[c][far, pl.ds(f, GROUP)])
    reduce_send(slots - 1)
    for key in sent:
        send_copy(key, *key).wait_send()
    for o in range(slots):
        for d in range(1, groups):
            reduce_copy(d, o).wait()
    for s in range(slots):
        column = lax.rem(me - off_ref[s, me] + tiles, tiles)
        col_ref[pl.ds(s, 1)] = table_ref[pl.ds(column, 1)]
        o = place[s]
        total = acc[o, :, pl.ds(grp * share, share), :].reshape(pairs * share, width)
        for d in range(1, groups):
            total = total + in_buf[d - 1, o].astype(jnp.float32)
        out_ref[s] = total


def local(tiles, groups, amplitudes, integrals, virt_energy, pair_energy, offsets):
    tile_index = lax.axis_index("blk")
    group_index = lax.axis_index("grp")
    aux, width = integrals.shape[0], integrals.shape[2]
    pairs, slots = amplitudes.shape[1], amplitudes.shape[2]
    share = width // groups
    chunks = max(2, min(4, 32 // tiles))
    rows_of, cols_of = grid_of(tiles // 2)
    y, x = rows_of - 1, cols_of - 1
    n_sent = chunks * (2 * (1 + x + y) + 2 * x * y + 2 * (x + y + x * y))
    depth = aux // chunks
    summed, col_energy = pl.pallas_call(
        functools.partial(kernel, tiles, groups, chunks),
        out_shape=(
            jax.ShapeDtypeStruct((slots, pairs * share, width), jnp.float32),
            jax.ShapeDtypeStruct((slots, width), jnp.float32),
        ),
        in_specs=[
            pl.BlockSpec(memory_space=pltpu.SMEM),
        ]
        + [pl.BlockSpec(memory_space=pltpu.VMEM)] * 3,
        out_specs=(pl.BlockSpec(memory_space=pltpu.VMEM),) * 2,
        scratch_shapes=[pltpu.VMEM((tiles, depth, width, width), jnp.bfloat16)] * chunks
        + [
            pltpu.VMEM((slots, width, pairs * width), jnp.bfloat16),
            pltpu.VMEM((slots, pairs, width, width), jnp.float32),
            pltpu.VMEM((groups - 1, slots, pairs * share, width), jnp.bfloat16),
            pltpu.VMEM((groups - 1, slots, pairs * share, width), jnp.bfloat16),
            pltpu.SemaphoreType.DMA((n_sent,)),
            pltpu.SemaphoreType.DMA((tiles, chunks, 2)),
            pltpu.SemaphoreType.DMA((groups - 1, slots)),
            pltpu.SemaphoreType.DMA((groups - 1, slots)),
        ],
        compiler_params=pltpu.CompilerParams(
            collective_id=0, has_side_effects=True, vmem_limit_bytes=56 << 20
        ),
        cost_estimate=pl.CostEstimate(
            flops=4 * aux * slots * pairs * width**3,
            bytes_accessed=4 << 20,
            transcendentals=0,
        ),
    )(offsets.T, virt_energy.reshape(tiles, width), amplitudes, integrals)
    ladder = summed.reshape(slots, pairs, share, width).transpose(2, 1, 0, 3)

    first_row = group_index * share
    old_rows = lax.dynamic_slice_in_dim(amplitudes, first_row, share, 0).astype(jnp.float32)
    row_energy = lax.dynamic_slice_in_dim(virt_energy, tile_index * width + first_row, share, 0)
    denom = (
        row_energy[:, None, None, None]
        + col_energy[None, None, :, :]
        - pair_energy[None, :, None, None]
    )
    return ladder, old_rows - ladder / denom


def solution(mesh):
    placed = (P("blk", None, None, None), P("grp", "blk", None), P(), P(), P())
    return jax.shard_map(
        functools.partial(local, mesh.shape["blk"], mesh.shape["grp"]),
        mesh=mesh,
        in_specs=placed,
        out_specs=(P(("blk", "grp"), None, None, None), P(("blk", "grp"), None, None, None)),
        check_vma=False,
    )
```
